256 devices in a mesh: outer: 8 (over z_lo, core), inner: 32 (over y, x, z_hi).
Axes of the slice: x: 4, y: 4, z: 8 (z_hi: 2, z_lo: 4; z = z_hi * 4 + z_lo), core: 2. Of those that a mesh axis runs over, the one named last changes fastest.
Arguments:
- cotangent: bfloat16 [32768, 2048], P(('outer', 'inner')), may hold values from -0.5 to 0.5
- hidden: bfloat16 [32768, 8, 384], P(('outer', 'inner')), may hold values from -24 to 24
- probs: float32 [32768, 8], P(('outer', 'inner')), may hold values from 0.02 to 0.5
- expert_ids: int32 [32768, 8], P(('outer', 'inner')), may hold values from 0 to 63, all different within a row; in each aligned block of 128 rows (0 to 127, 128 to 255, ...) at most 24 rows name the same one
- secondary: bfloat16 [384, 64, 2048], P(None, 'inner'), may hold values from -0.3125 to 0.3125
- weight: float32 [384, 64, 2048], P('outer', 'inner'), may hold values from -0.3125 to 0.3125
- moment1: float32 [384, 64, 2048], P('outer', 'inner'), may hold values from -4 to 4
- moment2: float32 [384, 64, 2048], P('outer', 'inner'), may hold values from 0.05 to 2
Outputs:
- d_hidden: bfloat16 [32768, 8, 384], P(('outer', 'inner'))
- d_probs: float32 [32768, 8], P(('outer', 'inner'))
- new_weight: float32 [384, 64, 2048], P('outer', 'inner')
- new_moment1: float32 [384, 64, 2048], P('outer', 'inner')
- new_moment2: float32 [384, 64, 2048], P('outer', 'inner')
- new_secondary: bfloat16 [384, 64, 2048], P(None, 'inner')
The draws below stay inside these ranges and needn't reach their ends.
Inputs may be any that keep to these rules, and one draw needn't show every extreme that they name: `expert_ids`: each token names 8 different experts. Among the 1024 choices of the rows of one device (aligned blocks of 128 tokens), no expert is named more than 24 times, a bound that some block reaches.
All inputs are finite; a program needn't handle non-finite values.
Results may differ from the reference program's by a relative error of at most 0.0085.
Values may be sent and summed in bfloat16 or wider, within the bound.
A program may use at most 128 MiB of HBM per device.

```python
import math
import jax
import jax.numpy as jnp
import numpy as np
from jax import lax

D = 2048
H = 384
EXPERTS = 64
TOP = 8
TOK_DEV = 128
CAP = 24
TOKENS = 32768
N_OUTER = 8
N_INNER = 32


def spiked(drawn, rng, source, target, parts, factor):
    def block_of(axis_at):
        return (jnp.arange(drawn.shape[axis_at]) // (drawn.shape[axis_at] // parts)).reshape((-1,) + (1,) * (drawn.ndim - 1 - axis_at))

    near = jax.random.permutation(rng, parts)[block_of(target)]
    second = (block_of(target) + parts // 2) % parts
    return jnp.where((block_of(source) == near) | (block_of(source) == second), factor * drawn, drawn)


def shard_levels(stream_key, extent, pieces, least, largest):
    level = 1.0
    for dim, shards_of in pieces:
        draws = jax.random.uniform(jax.random.fold_in(jax.random.fold_in(stream_key, 6), dim), (shards_of,), jnp.float32, least / len(pieces), largest / len(pieces))
        level = level * jnp.repeat(jnp.exp(draws), extent[dim] // shards_of).reshape((-1,) + (1,) * (len(extent) - 1 - dim))
    return level


def routed_block(own_key, own, number, rows, number_of, top, most, skew):
    order = jax.random.permutation(own_key, number_of)
    crowded, common = shares(number_of, rows * top, most, skew, True), shares(number_of, rows * top, most, skew, False)
    places = jnp.arange(number_of)

    def named(tallies, turn):
        used = int((tallies > 0).sum())
        fixed = max(1, used // 4)
        moved = fixed + (places - fixed + turn * (used - fixed)) % max(1, number_of - fixed)
        return jnp.zeros((number_of,), jnp.int32).at[order[jnp.where(places < fixed, places, moved)]].set(jnp.asarray(tallies, jnp.int32))

    tallies = jnp.where(number % 4 == 0, named(crowded, number // 4), named(common, number - number // 4 - 1))
    mixed = jax.random.permutation(jax.random.fold_in(own, 3), number_of)
    giver, taker = mixed[0:number_of // 2 * 2:2], mixed[1:number_of // 2 * 2:2]
    slack = jnp.minimum(tallies[giver] - 1, most - tallies[taker]) // 2
    slack = jnp.where((giver == order[0]) | (taker == order[0]) | (tallies[taker] == 0), 0, jnp.maximum(slack, 0))
    moved = jax.random.randint(jax.random.fold_in(own, 4), (number_of // 2,), 0, 1 << 20) % (slack + 1)
    tallies = tallies.at[giver].add(-moved).at[taker].add(moved)
    items = jnp.searchsorted(jnp.cumsum(tallies), jnp.arange(rows * top), side="right").astype(jnp.int32)
    table = items.reshape(top, rows).T
    table = table[jax.random.permutation(jax.random.fold_in(own, 1), rows)]
    turn = jax.random.randint(jax.random.fold_in(own, 2), (rows, 1), 0, top)
    return jnp.take_along_axis(table, (jnp.arange(top)[None, :] + turn) % top, axis=1)


def shares(amount, total, limit, slope, full):
    loads = [(1 << 20) // math.isqrt(grade ** slope) + 1 for grade in range(1, amount + 1)]
    largest = limit if full else min(limit, max(-(-total // amount), total * loads[0] // sum(loads)))
    least = 1 if total - largest >= amount - 1 else 0
    holding, spare = [largest] + [least] * (amount - 1), total - largest - least * (amount - 1)
    while spare > 0:
        movable = [i for i in range(1, amount) if holding[i] < largest] or [i for i in range(1, amount) if holding[i] < limit]
        whole, budget = sum([loads[i] for i in movable]), spare
        for i in movable:
            addition = min(limit - holding[i], max(1, budget * loads[i] // whole), spare)
            holding[i] = holding[i] + addition
            spare = spare - addition
    return np.array(holding)


def bell_draw(key, shape, spread, limit, split=(), kind=jnp.bfloat16):
    loudness = shard_levels(key, shape, split, -0.22, 0.18) if split else 1.0
    array = jax.random.normal(key, shape, jnp.float32) * spread * loudness
    return jnp.minimum(jnp.maximum(array, -limit), limit).astype(kind)


def bell_draw_with(key, extent, spread, most, pieces, heavy, kind=jnp.bfloat16):
    array = spread * jax.random.normal(key, extent, jnp.float32)
    if pieces:
        array = array * shard_levels(key, extent, pieces, -0.22, 0.18)
    return jnp.clip(spiked(array, jax.random.fold_in(key, 3), *heavy), -most, most).astype(kind)


def setup_inputs(seed: int = 0) -> dict:
    arg_keys = jax.random.split(jax.random.key(seed), 9)
    cotangent = bell_draw(arg_keys[0], (TOKENS, D), (TOKENS // 256) ** -0.5, 0.5, ((0, 256),))
    hidden = bell_draw_with(arg_keys[1], (TOKENS, TOP, H), 1.0, 24.0, ((0, 256),), (0, 2, 128, 5.5))
    probs = jnp.clip(jnp.exp(math.log(0.5) - 3.218876 * jax.random.uniform(arg_keys[2], (TOKENS, TOP), jnp.float32) ** shard_levels(arg_keys[2], (TOKENS, TOP), ((0, 256),), -0.2, 0.2)), 0.02, 0.5)
    expert_ids_keys = jax.random.split(jax.random.fold_in(arg_keys[3], 1), TOKENS // TOK_DEV)
    expert_ids_turns = jax.random.permutation(jax.random.fold_in(arg_keys[3], 3), TOKENS // TOK_DEV)
    expert_ids = jax.vmap(lambda own, number: routed_block(jax.random.fold_in(arg_keys[3], 2), own, number, TOK_DEV, EXPERTS, TOP, CAP, 0))(expert_ids_keys, expert_ids_turns).reshape((TOKENS, TOP))
    secondary = bell_draw(arg_keys[4], (H, EXPERTS, D), H ** -0.5, 0.3125, ((1, 32),))
    weight = bell_draw(arg_keys[5], (H, EXPERTS, D), H ** -0.5, 0.3125, ((0, 8), (1, 32)), jnp.float32)
    moment1 = bell_draw(arg_keys[6], (H, EXPERTS, D), 0.5, 4.0, ((0, 8), (1, 32)), jnp.float32)
    moment2 = jnp.clip(jnp.exp(math.log(2.0) - 3.6888794 * jax.random.uniform(arg_keys[7], (H, EXPERTS, D), jnp.float32) ** shard_levels(arg_keys[7], (H, EXPERTS, D), ((0, 8), (1, 32)), -0.2, 0.2)), 0.05, 2.0)
    return dict(cotangent=cotangent, hidden=hidden, probs=probs, expert_ids=expert_ids, secondary=secondary, weight=weight, moment1=moment1, moment2=moment2)


beta_one = 0.9
beta_two = 0.95
adam_epsilon = 1e-08
learn_rate = 0.003
decay_rate = 0.1
bias_one = 1.0 - 0.9 ** 20
bias_two = 1.0 - 0.95 ** 20

def slot_table(flat_ids):
    count = flat_ids.shape[0]
    onehot = (jnp.arange(EXPERTS, dtype=jnp.int32)[:, None] == flat_ids[None, :]).astype(jnp.int32)
    ranking = jnp.cumsum(onehot, axis=1) - onehot
    position = lax.optimization_barrier(jnp.sum(ranking * onehot, axis=0))
    target = flat_ids * CAP + position
    order = jnp.arange(count, dtype=jnp.int32)
    inverse = jnp.zeros((EXPERTS * CAP,), jnp.int32).at[target].set(order)
    filled = jnp.zeros((EXPERTS * CAP,), jnp.int32).at[target].set(1)
    return (target, inverse, filled)

def reference(cotangent, hidden, probs, expert_ids, secondary, weight, moment1, moment2):
    span = N_INNER * TOK_DEV
    per_device = TOK_DEV * TOP
    second_f = secondary.astype(jnp.float32)

    def group(total, index):
        start = (index * span).astype(jnp.int32)
        cot_rows = lax.dynamic_slice_in_dim(cotangent, start, span, 0).astype(jnp.float32)
        hid_rows = lax.dynamic_slice_in_dim(hidden, start, span, 0)
        prob_rows = lax.dynamic_slice_in_dim(probs, start, span, 0)
        id_rows = lax.dynamic_slice_in_dim(expert_ids, start, span, 0).reshape(N_INNER, per_device)
        target, inverse, filled = jax.vmap(slot_table)(id_rows)
        weighted = (prob_rows[..., None] * hid_rows.astype(jnp.float32)).astype(jnp.bfloat16)
        weighted = lax.optimization_barrier(weighted).astype(jnp.float32).reshape(N_INNER, per_device, H)
        source = jnp.arange(N_INNER, dtype=jnp.int32)[:, None]
        keep = filled.astype(jnp.float32)[..., None]
        w_slots = (weighted[source, inverse] * keep).reshape(N_INNER, EXPERTS, CAP, H)
        token_rows = source * TOK_DEV + inverse // TOP
        d_slots = (cot_rows[token_rows] * keep).reshape(N_INNER, EXPERTS, CAP, D)
        grads = jnp.einsum('jecd,hed->jech', d_slots, second_f).astype(jnp.bfloat16)
        partial_value = jnp.einsum('jech,jecd->hed', w_slots, d_slots)
        partial_value = lax.optimization_barrier(partial_value.astype(jnp.bfloat16)).astype(jnp.float32)
        back = lax.optimization_barrier(grads).astype(jnp.float32).reshape(N_INNER, EXPERTS * CAP, H)
        g_rows = back[source, target].reshape(span, TOP, H)
        d_hid = (prob_rows[..., None] * g_rows).astype(jnp.bfloat16)
        d_prob = lax.optimization_barrier(jnp.sum(hid_rows.astype(jnp.float32) * g_rows, axis=-1))
        return (total + partial_value, (d_hid, d_prob))
    grad, (d_hid, d_prob) = lax.scan(group, jnp.zeros((H, EXPERTS, D), jnp.float32), jnp.arange(N_OUTER, dtype=jnp.int32))
    d_hidden = d_hid.reshape(TOKENS, TOP, H)
    d_probs = d_prob.reshape(TOKENS, TOP)
    new_moment1 = beta_one * moment1 + (1.0 - beta_one) * grad
    new_moment2 = beta_two * moment2 + (1.0 - beta_two) * grad * grad
    update = new_moment1 / bias_one / (jnp.sqrt(new_moment2 / bias_two) + adam_epsilon) + decay_rate * weight
    new_weight = weight - learn_rate * update
    new_secondary = new_weight.astype(jnp.bfloat16)
    return (d_hidden, d_probs, new_weight, new_moment1, new_moment2, new_secondary)
```

```python
import functools

import jax
import jax.numpy as jnp
from jax import lax
from jax.experimental import pallas as pl
from jax.experimental.pallas import tpu as pltpu
from jax.sharding import PartitionSpec as P

EXPERTS = 64
CAP = 24
H = 384
D = 2048
NC = 4
CW = D // NC
MESH = pl.DeviceIdType.MESH
F32 = jnp.float32
BF16 = jnp.bfloat16

beta_one = 0.9
beta_two = 0.95
adam_epsilon = 1e-08
learn_rate = 0.003
decay_rate = 0.1
bias_one = 1.0 - 0.9**20
bias_two = 1.0 - 0.95**20


def body(
    cot_hbm, wsend, psend, sec_hbm, weight, moment1, moment2, tcol, pcol, hid,
    dh, dp, nw, nm1, nm2, ns,
    cot, sec, posr, wr, G, wT, M2, dsl, Pb, Ps, Rr, bs, br, TT, wv, m1v, m2v, nsv,
    loc, pos_s, pos_r, w_s, w_r, b_s, b_r, ag_s, ag_r, sc_s, sc_r, sd_s, sd_r,
    pd_s, pd_r, rs_s, rs_r, z_s, z_r, y_s, y_r,
):
    o = lax.axis_index("outer")
    i = lax.axis_index("inner")
    k = lax.rem(o, 2)
    zl = lax.div(o, 2)
    zh = lax.rem(i, 2)
    own = lax.div(i, 2)
    x = lax.rem(own, 4)
    y = lax.div(own, 4)
    z = zh * 4 + zl

    def dev(px, py, pz, pk):
        return (lax.rem(pz, 4) * 2 + pk, (py * 4 + px) * 2 + lax.div(pz, 4))

    def plane(p):
        return (o, p * 2 + zh)

    xp, xm = lax.rem(x + 1, 4), lax.rem(x + 3, 4)
    yp, ym = lax.rem(y + 1, 4), lax.rem(y + 3, 4)
    zp, zm = lax.rem(z + 1, 8), lax.rem(z + 7, 8)
    dxp, dxm = dev(xp, y, z, k), dev(xm, y, z, k)
    dyp, dym = dev(x, yp, z, k), dev(x, ym, z, k)
    dzp, dzm = dev(x, y, zp, k), dev(x, y, zm, k)
    sib = (zl * 2 + 1 - k, i)

    def remote(src, dst, ss, rs, where):
        return pltpu.make_async_remote_copy(
            src_ref=src, dst_ref=dst, send_sem=ss, recv_sem=rs, device_id=where, device_id_type=MESH
        )

    barrier = pltpu.get_barrier_semaphore()

    def hello(r, c):
        pl.semaphore_signal(
            barrier, inc=1, device_id=plane(lax.rem(own + r, 16)), device_id_type=MESH
        )
        return c

    lax.fori_loop(1, 16, hello, 0)
    for r in (1, 2, 3):
        pl.semaphore_signal(
            barrier, inc=1, device_id=(lax.rem(zl + r, 4) * 2 + k, i), device_id_type=MESH
        )
    for where in (sib, dzp, dzm):
        pl.semaphore_signal(barrier, inc=1, device_id=where, device_id_type=MESH)

    locals_ = [
        pltpu.make_async_copy(cot_hbm, cot.at[y, x], loc.at[0]),
        pltpu.make_async_copy(sec_hbm, sec.at[pl.ds(zh * 2, 2)], loc.at[1]),
        pltpu.make_async_copy(wsend.at[own], wr.at[own], loc.at[2]),
        pltpu.make_async_copy(psend.at[own], posr.at[own], loc.at[3]),
        pltpu.make_async_copy(weight, wv, loc.at[4]),
        pltpu.make_async_copy(moment1, m1v, loc.at[5]),
        pltpu.make_async_copy(moment2, m2v, loc.at[6]),
    ]
    for cp in locals_:
        cp.start()
    pl.semaphore_wait(barrier, 21)

    def cols(c):
        return pl.ds(c * CW, CW)

    def pos_copy(r, p):
        return remote(psend.at[p], posr.at[own], pos_s.at[r], pos_r.at[r], plane(p))

    def w_copy(r, p):
        return remote(wsend.at[p], wr.at[own], w_s.at[r], w_r.at[r], plane(p))

    def back_copy(r, p):
        return remote(bs.at[p], br.at[own], b_s.at[r], b_r.at[r], plane(p))

    A, B = pl.ds(0, 64), pl.ds(64, 64)
    A0, A1, B0, B1 = pl.ds(0, 32), pl.ds(32, 32), pl.ds(64, 32), pl.ds(96, 32)

    def gather_send(c, n):
        q = cols(c)
        spec = (
            (cot_hbm.at[A, q], cot.at[y, x, A, q], dxp),
            (cot_hbm.at[A, q], cot.at[y, x, A, q], dxm),
            (cot_hbm.at[B, q], cot.at[y, x, B, q], dyp),
            (cot_hbm.at[B, q], cot.at[y, x, B, q], dym),
            (cot.at[y, xm, A0, q],) * 2 + (dxp,),
            (cot.at[y, xp, A1, q],) * 2 + (dxm,),
            (cot.at[ym, x, B0, q],) * 2 + (dyp,),
            (cot.at[yp, x, B1, q],) * 2 + (dym,),
            (cot.at[y, :, A, q],) * 2 + (dyp,),
            (cot.at[y, :, A, q],) * 2 + (dym,),
            (cot.at[:, x, B, q],) * 2 + (dxp,),
            (cot.at[:, x, B, q],) * 2 + (dxm,),
            (cot.at[ym, :, A0, q],) * 2 + (dyp,),
            (cot.at[yp, :, A1, q],) * 2 + (dym,),
            (cot.at[:, xm, B0, q],) * 2 + (dxp,),
            (cot.at[:, xp, B1, q],) * 2 + (dxm,),
        )[n]
        return remote(spec[0], spec[1], ag_s.at[c, n], ag_r.at[c, n], spec[2])

    def g_start(c, stage):
        for n in range(4 * stage, 4 * stage + 4):
            gather_send(c, n).start()

    def g_wait(c, stage):
        for n in range(4 * stage, 4 * stage + 4):
            gather_send(c, n).wait_recv()

    q_up = 1 - lax.div(zp, 4)
    q_dn = 1 - lax.div(zm, 4)
    other = 1 - zh
    R0_, R1_ = pl.ds(0, 192), pl.ds(192, 192)

    def chain(c, way):
        q = cols(c)
        ref = sec.at[q_up * 2 + k, R0_, q] if way == 0 else sec.at[q_dn * 2 + k, R1_, q]
        return remote(ref, ref, sc_s.at[c, way], sc_r.at[c, way], dzp if way == 0 else dzm)

    def chain_sib(c, way):
        ref = sec.at[other * 2 + k, R0_ if way == 0 else R1_, cols(c)]
        return remote(ref, ref, sd_s.at[c, way], sd_r.at[c, way], sib)

    def chain_begin():
        locals_[1].wait()

        @pl.when(zl == 3)
        def _():
            for c in range(NC):
                chain(c, 0).start()

        @pl.when(zl == 0)
        def _():
            for c in range(NC):
                chain(c, 1).start()

    def chain_step(c):
        chain(c, 0).wait_recv()

        @pl.when(zl < 3)
        def _():
            chain(c, 0).start()

        chain_sib(c, 0).start()
        chain(c, 1).wait_recv()

        @pl.when(zl > 0)
        def _():
            chain(c, 1).start()

        chain_sib(c, 1).start()

    def chain_end(c):
        chain_sib(c, 0).wait_recv()
        chain_sib(c, 1).wait_recv()

    def build_TT():
        def one(b, carry):
            rows = pl.ds(b * 128, 128)
            t = tcol[rows, :]
            slot = lax.broadcasted_iota(jnp.int32, (128, EXPERTS * CAP), 1)
            TT[rows, :] = jnp.where(slot == t, 1.0, 0.0).astype(BF16)
            return carry

        lax.fori_loop(0, 8, one, 0)

    def build_M2():
        def one(b, carry):
            j = lax.broadcasted_iota(jnp.int32, (CAP, 128), 0).astype(F32)
            zero = jnp.zeros((CAP, 128), F32)
            first, second = posr[2 * b], posr[2 * b + 1]
            rows = []
            for q in range(4):
                one_a = jnp.where(first[q : q + 1, :] == j, 1.0, 0.0)
                one_b = jnp.where(second[q : q + 1, :] == j, 1.0, 0.0)
                rows.append(jnp.concatenate([one_a, zero], axis=1))
                rows.append(jnp.concatenate([zero, one_b], axis=1))
            M2[b] = jnp.concatenate(rows, axis=0).astype(BF16)
            return carry

        lax.fori_loop(0, 8, one, 0)

    def build_wT():
        def one(s, carry):
            block = wr[s].astype(F32)
            for q in range(4):
                G[q, pl.ds(s * CAP, CAP), :] = block[q * CAP : (q + 1) * CAP, :]
            return carry

        lax.fori_loop(0, 16, one, 0)
        for q in range(4):
            wT[q] = jnp.transpose(G[q]).astype(BF16)

    def rows_of(c):
        q = cols(c)

        def one(b, carry):
            block = cot[lax.div(b, 2), pl.ds(lax.rem(b, 2) * 2, 2), :, q].reshape(256, CW)
            got = jnp.dot(M2[b], block, preferred_element_type=F32).astype(BF16)
            for e in range(4):
                dsl[e, pl.ds(b * 48, 48), :] = got[e * 48 : (e + 1) * 48, :]
            return carry

        lax.fori_loop(0, 8, one, 0)

    def partials(c):
        for e in range(4):
            got = jnp.dot(wT[e], dsl[e], preferred_element_type=F32).astype(BF16)
            for s in range(8):
                Pb[c, s % 2, (e // 2) * 4 + s // 2, e % 2] = got[s * 48 : (s + 1) * 48, :]

    def hidden_grads(c):
        for e in range(4):
            got = lax.dot_general(
                dsl[e], sec[e, :, cols(c)], (((1,), (1,)), ((), ())), preferred_element_type=F32
            )
            G[e] = got if c == 0 else G[e] + got

    def pair_copy(c):
        return remote(Pb.at[c, 1 - k], Ps.at[c], pd_s.at[c], pd_r.at[c], sib)

    def ring_copy(c, t, way):
        far = 4 - t
        d = lax.rem(z + far, 8) if way == 0 else lax.rem(z + 8 - far, 8)
        where = dzp if way == 0 else dzm
        if t == 0:
            src, dst = Pb.at[c, k, d, way], Rr.at[c, t, way, way]
        else:
            src, dst = Pb.at[c, k, d], Rr.at[c, t, way]
        return remote(src, dst, rs_s.at[c, t, way], rs_r.at[c, t, way], where)

    def pair_sum(c):
        pair_copy(c).wait_recv()
        Pb[c, k] = (Pb[c, k].astype(F32) + Ps[c].astype(F32)).astype(BF16)
        ring_copy(c, 0, 0).start()
        ring_copy(c, 0, 1).start()

    def ring_step(c, t):
        for way in range(2):
            far = 4 - t
            d = lax.rem(z + far, 8) if way == 0 else lax.rem(z + 8 - far, 8)
            ring_copy(c, t - 1, way).wait_recv()
            if t == 1:
                Pb[c, k, d, way] = (
                    Pb[c, k, d, way].astype(F32) + Rr[c, 0, way, way].astype(F32)
                ).astype(BF16)
            else:
                Pb[c, k, d] = (Pb[c, k, d].astype(F32) + Rr[c, t - 1, way].astype(F32)).astype(BF16)
            ring_copy(c, t, way).start()

    def z_copy(c, r):
        src = nsv.at[:, :, cols(c)]
        dst = ns.at[2 * zl + k, :, :, cols(c)]
        return remote(src, dst, z_s.at[c, r], z_r.at[c, r], (lax.rem(zl + r, 4) * 2 + k, i))

    def y_copy(c, r):
        home = 2 * lax.rem(zl + 4 - r, 4) + k
        dst = ns.at[home, :, :, cols(c)]
        src = nsv.at[:, :, cols(c)] if r == 0 else dst
        return remote(src, dst, y_s.at[c, r], y_r.at[c, r], sib)

    def own_copy(c):
        return pltpu.make_async_copy(
            nsv.at[:, :, cols(c)], ns.at[2 * zl + k, :, :, cols(c)], loc.at[7 + c]
        )

    def out_copies(c):
        q = cols(c)
        return [
            pltpu.make_async_copy(v.at[:, :, q], dst.at[:, :, q], loc.at[7 + NC + 3 * c + n])
            for n, (v, dst) in enumerate(((wv, nw), (m1v, nm1), (m2v, nm2)))
        ]

    def adam(c):
        q = cols(c)
        if c == 0:
            for cp in locals_[4:]:
                cp.wait()
        ring_copy(c, 3, 0).wait_recv()
        ring_copy(c, 3, 1).wait_recv()
        grad = Pb[c, k, z].astype(F32) + Rr[c, 3, 0].astype(F32) + Rr[c, 3, 1].astype(F32)
        w = wv[:, :, q]
        a = beta_one * m1v[:, :, q] + (1.0 - beta_one) * grad
        b = beta_two * m2v[:, :, q] + (1.0 - beta_two) * grad * grad
        update = a / bias_one / (jnp.sqrt(b / bias_two) + adam_epsilon) + decay_rate * w
        w = w - learn_rate * update
        wv[:, :, q] = w
        m1v[:, :, q] = a
        m2v[:, :, q] = b
        nsv[:, :, q] = w.astype(BF16)
        for r in (1, 2, 3):
            z_copy(c, r).start()
        y_copy(c, 0).start()
        own_copy(c).start()
        for cp in out_copies(c):
            cp.start()

    def z_forward(c):
        for r in (1, 3, 2):
            z_copy(c, r).wait_recv()
            y_copy(c, r).start()

    def z_end(c):
        for r in range(4):
            y_copy(c, r).wait_recv()

    def send_back():
        def one(r, carry):
            s = lax.rem(own + r, 16)
            rows = [G[e, pl.ds(s * CAP, CAP), :] for e in range(4)]
            bs[s] = jnp.concatenate(rows, axis=0).astype(BF16)

            @pl.when(r < 16)
            def _():
                back_copy(r, s).start()

            return carry

        lax.fori_loop(1, 17, one, 0)
        pltpu.make_async_copy(bs.at[own], br.at[own], loc.at[7 + 4 * NC]).start()

    def finish():
        pltpu.make_async_copy(bs.at[own], br.at[own], loc.at[7 + 4 * NC]).wait()

        def arrive(r, carry):
            p = lax.rem(own + 16 - r, 16)
            remote(br.at[p], br.at[p], b_s.at[r], b_r.at[r], plane(p)).wait_recv()
            return carry

        lax.fori_loop(1, 16, arrive, 0)

        def one(b, carry):
            rows = pl.ds(b * 128, 128)
            g = jnp.dot(
                TT[rows, :], br[...].reshape(EXPERTS * CAP, H), preferred_element_type=F32
            )
            dh[rows, :] = (pcol[rows, :] * g).astype(BF16)
            dp[rows, :] = jnp.sum(hid[rows, :].astype(F32) * g, axis=1, keepdims=True)
            return carry

        lax.fori_loop(0, 8, one, 0)

    def send_rows(r, carry):
        p = lax.rem(own + r, 16)
        pos_copy(r, p).start()
        w_copy(r, p).start()
        return carry

    def pos_arrive(r, carry):
        p = lax.rem(own + 16 - r, 16)
        remote(posr.at[p], posr.at[p], pos_s.at[r], pos_r.at[r], plane(p)).wait_recv()
        return carry

    def w_arrive(r, carry):
        p = lax.rem(own + 16 - r, 16)
        remote(wr.at[p], wr.at[p], w_s.at[r], w_r.at[r], plane(p)).wait_recv()
        return carry

    g_start(0, 0)
    lax.fori_loop(1, 16, send_rows, 0)
    chain_begin()
    for c in range(1, NC):
        g_start(c, 0)
    build_TT()
    locals_[0].wait()
    g_wait(0, 0)
    g_start(0, 1)
    g_wait(0, 1)
    g_start(0, 2)
    lax.fori_loop(1, 16, pos_arrive, 0)
    locals_[3].wait()
    build_M2()
    g_wait(1, 0)
    g_start(1, 1)
    g_wait(0, 2)
    g_start(0, 3)
    g_wait(1, 1)
    g_start(1, 2)
    chain_step(0)
    lax.fori_loop(1, 16, w_arrive, 0)
    locals_[2].wait()
    build_wT()

    for c in range(NC):
        g_wait(c, 3)
        rows_of(c)
        if c + 2 < NC:
            g_wait(c + 2, 0)
            g_start(c + 2, 1)
        partials(c)
        pair_copy(c).start()
        if c + 1 < NC:
            g_wait(c + 1, 2)
            g_start(c + 1, 3)
            chain_step(c + 1)
        if c + 2 < NC:
            g_wait(c + 2, 1)
            g_start(c + 2, 2)
        if c >= 1:
            ring_step(c - 1, 1)
        chain_end(c)
        hidden_grads(c)
        if c == NC - 1:
            send_back()
        if c >= 1:
            ring_step(c - 1, 2)
        if c >= 2:
            adam(c - 2)
        pair_sum(c)
        if c >= 1:
            ring_step(c - 1, 3)
        if c >= 3:
            z_forward(c - 3)
    c = NC - 1
    ring_step(c, 1)
    adam(c - 1)
    ring_step(c, 2)
    z_forward(c - 2)
    ring_step(c, 3)
    z_forward(c - 1)
    adam(c)
    finish()
    z_forward(c)
    for c in range(NC):
        z_end(c)

    def sent(r, carry):
        p = lax.rem(own + r, 16)
        pos_copy(r, p).wait_send()
        w_copy(r, p).wait_send()
        back_copy(r, p).wait_send()
        return carry

    lax.fori_loop(1, 16, sent, 0)
    for c in range(NC):
        for n in range(16):
            gather_send(c, n).wait_send()
        for way in range(2):
            chain_sib(c, way).wait_send()
            for t in range(4):
                ring_copy(c, t, way).wait_send()
        chain(c, 0).wait_send()
        chain(c, 1).wait_send()
        pair_copy(c).wait_send()
        for r in range(4):
            if r:
                z_copy(c, r).wait_send()
            y_copy(c, r).wait_send()
        own_copy(c).wait()
        for cp in out_copies(c):
            cp.wait()


def slot_targets(expert_ids):
    experts = jnp.arange(EXPERTS, dtype=jnp.int32)
    ids = expert_ids.T
    chosen = jnp.any(ids[:, None, :] == experts[None, :, None], axis=0)
    before = (jnp.arange(128)[:, None] < jnp.arange(128)[None, :]).astype(BF16)
    rank = jnp.dot(chosen.astype(BF16), before, preferred_element_type=F32)
    pos = jnp.where(chosen, rank, -1.0)
    place = rank + (experts * CAP).astype(F32)[:, None]
    target = jnp.sum(
        jnp.where(ids[:, None, :] == experts[None, :, None], place[None], 0.0), axis=1
    )
    return pos, target.T.astype(jnp.int32).reshape(1024)


def local(cotangent, hidden, probs, expert_ids, secondary, weight, moment1, moment2):
    pos, target = slot_targets(expert_ids)
    pcol = probs.reshape(1024, 1)
    hid = hidden.reshape(1024, H)
    weighted = (pcol * hid.astype(F32)).astype(BF16)
    slots = jnp.arange(EXPERTS * CAP, dtype=jnp.int32)
    matches = (slots[:, None] == target[None, :]).astype(BF16)
    wsend = jnp.dot(matches, weighted, preferred_element_type=F32).astype(BF16)
    wsend = wsend.reshape(16, 4 * CAP, H)
    psend = jnp.concatenate([pos.reshape(16, 4, 128), jnp.zeros((16, 4, 128), F32)], axis=1)
    tcol = target.reshape(1024, 1)
    sec = secondary.transpose(1, 0, 2)
    wt, m1, m2 = (a.transpose(1, 0, 2) for a in (weight, moment1, moment2))

    hbm = pl.BlockSpec(memory_space=pl.ANY)
    vmem = pl.BlockSpec(memory_space=pltpu.VMEM)
    dma = pltpu.SemaphoreType.DMA
    shape = jax.ShapeDtypeStruct
    dh, dp, nw, nm1, nm2, ns = pl.pallas_call(
        body,
        out_shape=(
            shape((1024, H), BF16),
            shape((1024, 1), F32),
            shape((2, 48, D), F32),
            shape((2, 48, D), F32),
            shape((2, 48, D), F32),
            shape((8, 2, 48, D), BF16),
        ),
        in_specs=[hbm] * 7 + [vmem] * 3,
        out_specs=(vmem, vmem, hbm, hbm, hbm, hbm),
        scratch_shapes=[
            pltpu.VMEM((4, 4, 128, D), BF16),
            pltpu.VMEM((4, H, D), BF16),
            pltpu.VMEM((16, 8, 128), F32),
            pltpu.VMEM((16, 4 * CAP, H), BF16),
            pltpu.VMEM((4, H, H), F32),
            pltpu.VMEM((4, H, H), BF16),
            pltpu.VMEM((8, 192, 256), BF16),
            pltpu.VMEM((4, H, CW), BF16),
            pltpu.VMEM((NC, 2, 8, 2, 48, CW), BF16),
            pltpu.VMEM((NC, 8, 2, 48, CW), BF16),
            pltpu.VMEM((NC, 4, 2, 2, 48, CW), BF16),
            pltpu.VMEM((16, 4 * CAP, H), BF16),
            pltpu.VMEM((16, 4 * CAP, H), BF16),
            pltpu.VMEM((1024, EXPERTS * CAP), BF16),
            pltpu.VMEM((2, 48, D), F32),
            pltpu.VMEM((2, 48, D), F32),
            pltpu.VMEM((2, 48, D), F32),
            pltpu.VMEM((2, 48, D), BF16),
            dma((8 + 4 * NC,)),
            dma((16,)), dma((16,)), dma((16,)), dma((16,)), dma((16,)), dma((16,)),
            dma((NC, 16)), dma((NC, 16)),
            dma((NC, 2)), dma((NC, 2)), dma((NC, 2)), dma((NC, 2)),
            dma((NC,)), dma((NC,)),
            dma((NC, 4, 2)), dma((NC, 4, 2)),
            dma((NC, 4)), dma((NC, 4)), dma((NC, 4)), dma((NC, 4)),
        ],
        compiler_params=pltpu.CompilerParams(
            collective_id=0, has_side_effects=True, vmem_limit_bytes=60 * 1024 * 1024
        ),
    )(cotangent, wsend, psend, sec, wt, m1, m2, tcol, pcol, hid)
    nw, nm1, nm2 = (a.transpose(1, 0, 2) for a in (nw, nm1, nm2))
    ns = ns.transpose(0, 2, 1, 3).reshape(H, 2, D)
    return dh.reshape(128, 8, H), dp.reshape(128, 8), nw, nm1, nm2, ns


def solution(mesh):
    in_specs = (
        P(("outer", "inner"), None),
        P(("outer", "inner"), None, None),
        P(("outer", "inner"), None),
        P(("outer", "inner"), None),
        P(None, "inner", None),
        P("outer", "inner", None),
        P("outer", "inner", None),
        P("outer", "inner", None),
    )
    out_specs = (
        P(("outer", "inner"), None, None),
        P(("outer", "inner"), None),
        P("outer", "inner", None),
        P("outer", "inner", None),
        P("outer", "inner", None),
        P(None, "inner", None),
    )
    return jax.shard_map(local, mesh=mesh, in_specs=in_specs, out_specs=out_specs, check_vma=False)
```

```python
import functools

import jax
import jax.numpy as jnp
from jax import lax
from jax.experimental import pallas as pl
from jax.experimental.pallas import tpu as pltpu
from jax.sharding import PartitionSpec as P

EXPERTS = 64
CAP = 24
H = 384
D = 2048
NC = 8
CW = D // NC
MESH = pl.DeviceIdType.MESH
F32 = jnp.float32
BF16 = jnp.bfloat16

beta_one = 0.9
beta_two = 0.95
adam_epsilon = 1e-08
learn_rate = 0.003
decay_rate = 0.1
bias_one = 1.0 - 0.9**20
bias_two = 1.0 - 0.95**20


def body(
    cot_hbm, ids, prT, hid_hbm, sec_hbm, weight, moment1, moment2,
    dh, dpT, nw, nm1, nm2, ns,
    cot, sec, ps, posr, ws, wr, G, wT, M2, dsl, Pb, Ps, Rr, bs, br, TT, T, Wk, hid, outf,
    tgt, tgc, pc, wv, m1v, m2v, nsx,
    loc, in_s, out_s, pos_s, pos_r, w_s, w_r, b_s, b_r, ag_s, ag_r, sc_s, sc_r, sd_s, sd_r,
    pd_s, pd_r, rs_s, rs_r, z_s, z_r, y_s, y_r,
):
    o = lax.axis_index("outer")
    i = lax.axis_index("inner")
    k = lax.rem(o, 2)
    zl = lax.div(o, 2)
    zh = lax.rem(i, 2)
    own = lax.div(i, 2)
    x = lax.rem(own, 4)
    y = lax.div(own, 4)
    z = zh * 4 + zl

    def dev(px, py, pz, pk):
        return (lax.rem(pz, 4) * 2 + pk, (py * 4 + px) * 2 + lax.div(pz, 4))

    def plane(p):
        return (o, p * 2 + zh)

    xp, xm = lax.rem(x + 1, 4), lax.rem(x + 3, 4)
    yp, ym = lax.rem(y + 1, 4), lax.rem(y + 3, 4)
    zp, zm = lax.rem(z + 1, 8), lax.rem(z + 7, 8)
    dxp, dxm = dev(xp, y, z, k), dev(xm, y, z, k)
    dyp, dym = dev(x, yp, z, k), dev(x, ym, z, k)
    dzp, dzm = dev(x, y, zp, k), dev(x, y, zm, k)
    sib = (zl * 2 + 1 - k, i)

    def remote(src, dst, ss, rs, where):
        return pltpu.make_async_remote_copy(
            src_ref=src, dst_ref=dst, send_sem=ss, recv_sem=rs, device_id=where, device_id_type=MESH
        )

    barrier = pltpu.get_barrier_semaphore()

    def hello(r, c):
        pl.semaphore_signal(
            barrier, inc=1, device_id=plane(lax.rem(own + r, 16)), device_id_type=MESH
        )
        return c

    lax.fori_loop(1, 16, hello, 0)
    for where in (sib, dzp, dzm):
        pl.semaphore_signal(barrier, inc=1, device_id=where, device_id_type=MESH)

    locals_ = [
        pltpu.make_async_copy(hid_hbm, hid, loc.at[2]),
        pltpu.make_async_copy(weight, wv, loc.at[4]),
        pltpu.make_async_copy(moment1, m1v, loc.at[5]),
        pltpu.make_async_copy(moment2, m2v, loc.at[6]),
    ]
    def cols(c):
        return pl.ds(c * CW if isinstance(c, int) else pl.multiple_of(c * CW, CW), CW)

    def cot_in(c):
        return pltpu.make_async_copy(cot_hbm.at[:, cols(c)], cot.at[y, x, c], in_s.at[0, c])

    def sec_in(c):
        return pltpu.make_async_copy(sec_hbm.at[:, :, cols(c)], sec.at[zh, c], in_s.at[1, c])

    for c in range(NC):
        cot_in(c).start()
        sec_in(c).start()
    for cp in locals_:
        cp.start()

    def rank_choices():
        named = ids[...]
        experts = lax.broadcasted_iota(jnp.int32, (EXPERTS, 128), 0)
        hits = [named[n : n + 1, :] == experts for n in range(8)]
        chosen = functools.reduce(jnp.logical_or, hits)
        first = lax.broadcasted_iota(jnp.int32, (128, 128), 0)
        second = lax.broadcasted_iota(jnp.int32, (128, 128), 1)
        before = jnp.where(first < second, 1.0, 0.0).astype(BF16)
        rank = jnp.dot(
            jnp.where(chosen, 1.0, 0.0).astype(BF16), before, preferred_element_type=F32
        )
        ps[...] = jnp.where(chosen, rank, -1.0).reshape(8, 8, 128)
        place = rank + (experts * CAP).astype(F32)
        rows = [jnp.sum(jnp.where(hit, place, 0.0), axis=0, keepdims=True) for hit in hits]
        target = jnp.concatenate(rows, axis=0)
        tgt[...] = target
        tgc[...] = jnp.transpose(target)
        pc[...] = jnp.transpose(prT[...])

    rank_choices()
    pl.semaphore_wait(barrier, 18)

    def pos_copy(r, p):
        return remote(ps.at[lax.div(p, 2)], posr.at[own], pos_s.at[r], pos_r.at[r], plane(p))

    def w_copy(r, p):
        return remote(ws.at[p], wr.at[own], w_s.at[r], w_r.at[r], plane(p))

    def back_copy(r, p):
        return remote(bs.at[p], br.at[own], b_s.at[r], b_r.at[r], plane(p))

    A, B = pl.ds(0, 64), pl.ds(64, 64)
    A0, A1, B0, B1 = pl.ds(0, 32), pl.ds(32, 32), pl.ds(64, 32), pl.ds(96, 32)

    def gather_send(c, n):
        q = cols(c)
        spec = (
            (cot_hbm.at[A, q], cot.at[y, x, c, A], dxp),
            (cot_hbm.at[A, q], cot.at[y, x, c, A], dxm),
            (cot_hbm.at[B, q], cot.at[y, x, c, B], dyp),
            (cot_hbm.at[B, q], cot.at[y, x, c, B], dym),
            (cot.at[y, xm, c, A0],) * 2 + (dxp,),
            (cot.at[y, xp, c, A1],) * 2 + (dxm,),
            (cot.at[ym, x, c, B0],) * 2 + (dyp,),
            (cot.at[yp, x, c, B1],) * 2 + (dym,),
            (cot.at[y, :, c, A],) * 2 + (dyp,),
            (cot.at[y, :, c, A],) * 2 + (dym,),
            (cot.at[:, x, c, B],) * 2 + (dxp,),
            (cot.at[:, x, c, B],) * 2 + (dxm,),
            (cot.at[ym, :, c, A0],) * 2 + (dyp,),
            (cot.at[yp, :, c, A1],) * 2 + (dym,),
            (cot.at[:, xm, c, B0],) * 2 + (dxp,),
            (cot.at[:, xp, c, B1],) * 2 + (dxm,),
        )[n]
        return remote(spec[0], spec[1], ag_s.at[c, n], ag_r.at[c, n], spec[2])

    def g_start(c, stage):
        if stage == 2:
            cot_in(c).wait()
        for n in range(4 * stage, 4 * stage + 4):
            gather_send(c, n).start()

    def g_wait(c, stage):
        for n in range(4 * stage, 4 * stage + 4):
            gather_send(c, n).wait_recv()

    q_up = 1 - lax.div(zp, 4)
    q_dn = 1 - lax.div(zm, 4)
    other = 1 - zh
    quarter = [pl.ds(pl.multiple_of((k * 2 + way) * 96, 96), 96) for way in range(2)]

    def chain(c, way):
        ref = sec.at[(q_up, q_dn)[way], c, quarter[way]]
        return remote(ref, ref, sc_s.at[c, way], sc_r.at[c, way], (dzp, dzm)[way])

    def chain_sib(c, way):
        ref = sec.at[other, c, quarter[way]]
        return remote(ref, ref, sd_s.at[c, way], sd_r.at[c, way], sib)

    def chain_begin(c):
        sec_in(c).wait()

        @pl.when(zl == 3)
        def _():
            chain(c, 0).start()

        @pl.when(zl == 0)
        def _():
            chain(c, 1).start()

    def chain_step(slot):
        up, dn = slot - zl, slot - 3 + zl

        @pl.when((up >= 0) & (up < NC))
        def _():
            chain(up, 0).wait_recv()

            @pl.when(zl < 3)
            def _():
                chain(up, 0).start()

            chain_sib(up, 0).start()

        @pl.when((dn >= 0) & (dn < NC))
        def _():
            chain(dn, 1).wait_recv()

            @pl.when(zl > 0)
            def _():
                chain(dn, 1).start()

            chain_sib(dn, 1).start()

    def chain_end(c):
        chain_sib(c, 0).wait_recv()
        chain_sib(c, 1).wait_recv()

    def choices():
        pltpu.make_async_copy(ps.at[lax.div(own, 2)], posr.at[own], loc.at[3]).start()

        def one(r, carry):
            pos_copy(r, lax.rem(own + r, 16)).start()
            return carry

        lax.fori_loop(1, 16, one, 0)

    def build_rows():
        def one(b, carry):
            rows = pl.ds(b * 128, 128)
            slot = (lax.broadcasted_iota(jnp.int32, (128, 128), 0) + b * 128).astype(F32)
            for n in range(8):
                hit = slot == tgt[n : n + 1, :]
                T[rows, n * 128 : (n + 1) * 128] = jnp.where(hit, 1.0, 0.0).astype(BF16)
            return carry

        lax.fori_loop(0, 12, one, 0)
        locals_[0].wait()
        for n in range(8):
            rows = pc[:, n : n + 1] * hid[:, n, :].astype(F32)
            Wk[n * 128 : (n + 1) * 128, :] = rows.astype(BF16)

    def send_rows(n):
        ry = lax.rem(y + n + 1, 4)
        rows = pl.ds(pl.multiple_of(ry * 384, 384), 384)
        block = jnp.dot(T[rows, :], Wk[...], preferred_element_type=F32)
        ws[pl.ds(ry * 4, 4)] = block.astype(BF16).reshape(4, 4 * CAP, H)
        for m in range(4):
            p = ry * 4 + lax.rem(x + m, 4)
            if n == 3 and m == 0:
                pltpu.make_async_copy(ws.at[own], wr.at[own], loc.at[8]).start()
            else:
                w_copy(lax.rem(p - own + 16, 16), p).start()

    def build_TT():
        slot = lax.broadcasted_iota(jnp.int32, (128, EXPERTS * CAP), 1).astype(F32)
        for n in range(8):
            hit = slot == tgc[:, n : n + 1]
            TT[n * 128 : (n + 1) * 128, :] = jnp.where(hit, 1.0, 0.0).astype(BF16)

    def build_M2():
        lax.fori_loop(1, 16, pos_arrive, 0)
        pltpu.make_async_copy(ps.at[lax.div(own, 2)], posr.at[own], loc.at[3]).wait()
        odd = lax.rem(own, 2) == 1

        def one(b, carry):
            j = lax.broadcasted_iota(jnp.int32, (CAP, 128), 0).astype(F32)
            zero = jnp.zeros((CAP, 128), F32)
            first, second = (
                jnp.where(odd, part[4:8, :], part[0:4, :])
                for part in (posr[2 * b], posr[2 * b + 1])
            )
            rows = []
            for q in range(4):
                one_a = jnp.where(first[q : q + 1, :] == j, 1.0, 0.0)
                one_b = jnp.where(second[q : q + 1, :] == j, 1.0, 0.0)
                rows.append(jnp.concatenate([one_a, zero], axis=1))
                rows.append(jnp.concatenate([zero, one_b], axis=1))
            M2[b] = jnp.concatenate(rows, axis=0).astype(BF16)
            return carry

        lax.fori_loop(0, 8, one, 0)

    def build_wT():
        lax.fori_loop(1, 16, w_arrive, 0)
        pltpu.make_async_copy(ws.at[own], wr.at[own], loc.at[8]).wait()

        def one(s, carry):
            block = wr[s].astype(F32)
            for q in range(4):
                G[q // 2, pl.ds(q % 2 * H + s * CAP, CAP), 0:H] = block[q * CAP : (q + 1) * CAP, :]
            return carry

        lax.fori_loop(0, 16, one, 0)
        for q in range(4):
            wT[q] = jnp.transpose(G[q // 2, q % 2 * H : q % 2 * H + H, 0:H]).astype(BF16)

    def rows_of(c):
        g_wait(c, 3)

        def one(b, carry):
            block = cot[lax.div(b, 2), pl.ds(lax.rem(b, 2) * 2, 2), c].reshape(256, CW)
            got = jnp.dot(M2[b], block, preferred_element_type=F32).astype(BF16)
            for e in range(4):
                dsl[e // 2, pl.ds(e % 2 * H + b * 48, 48), :] = got[e * 48 : (e + 1) * 48, :]
            return carry

        lax.fori_loop(0, 8, one, 0)

    def partials(c):
        for e in range(4):
            got = jnp.dot(
                wT[e], dsl[e // 2, e % 2 * H : e % 2 * H + H, :], preferred_element_type=F32).astype(BF16)
            for s in range(8):
                Pb[c, s % 2, (e // 2) * 4 + s // 2, e % 2] = got[s * 48 : (s + 1) * 48, :]
        pair_copy(c).start()

    def hidden_grads(c):
        chain_end(c)
        for e in range(4):
            rows = slice(e % 2 * H, e % 2 * H + H)
            got = lax.dot_general(
                dsl[e // 2, rows, :],
                sec[e // 2, c].reshape(2 * H, CW),
                (((1,), (1,)), ((), ())),
                preferred_element_type=F32,
            )
            G[e // 2, rows, :] = got if c == 0 else G[e // 2, rows, :] + got

    def pair_copy(c):
        return remote(Pb.at[c, 1 - k], Ps.at[c], pd_s.at[c], pd_r.at[c], sib)

    def ring_copy(c, t, way):
        far = 4 - t
        d = lax.rem(z + far, 8) if way == 0 else lax.rem(z + 8 - far, 8)
        where = dzp if way == 0 else dzm
        if t == 0:
            src, dst = Pb.at[c, k, d, way], Rr.at[c, t, way, way]
        else:
            src, dst = Pb.at[c, k, d], Rr.at[c, t, way]
        return remote(src, dst, rs_s.at[c, t, way], rs_r.at[c, t, way], where)

    def pair_sum(c):
        pair_copy(c).wait_recv()
        Pb[c, k] = (Pb[c, k].astype(F32) + Ps[c].astype(F32)).astype(BF16)
        ring_copy(c, 0, 0).start()
        ring_copy(c, 0, 1).start()

    def ring_step(c, t):
        for way in range(2):
            far = 4 - t
            d = lax.rem(z + far, 8) if way == 0 else lax.rem(z + 8 - far, 8)
            ring_copy(c, t - 1, way).wait_recv()
            if t == 1:
                Pb[c, k, d, way] = (
                    Pb[c, k, d, way].astype(F32) + Rr[c, 0, way, way].astype(F32)
                ).astype(BF16)
            else:
                Pb[c, k, d] = (Pb[c, k, d].astype(F32) + Rr[c, t - 1, way].astype(F32)).astype(BF16)
            ring_copy(c, t, way).start()

    def z_copy(c, way, j):
        shard = jnp.maximum(zl - j, 0) if way == 0 else jnp.minimum(zl + j, 3)
        ref = nsx.at[c, 2 * shard + k]
        return remote(ref, ref, z_s.at[c, way, j], z_r.at[c, way, j], (dzp, dzm)[way])

    def z_sends(way, j):
        return ((zl >= j) & (zl < 3)) if way == 0 else ((zl + j <= 3) & (zl > 0))

    def y_copy(c, shard):
        ref = nsx.at[c, 2 * shard + k]
        return remote(ref, ref, y_s.at[c, shard], y_r.at[c, shard], sib)

    def ns_out(c):
        return pltpu.make_async_copy(nsx.at[c], ns.at[:, :, :, cols(c)], out_s.at[c])

    def out_copies(c):
        q = cols(c)
        return [
            pltpu.make_async_copy(v.at[:, :, q], dst.at[:, :, q], loc.at[9 + 3 * c + n])
            for n, (v, dst) in enumerate(((wv, nw), (m1v, nm1), (m2v, nm2)))
        ]

    def adam(c):
        q = cols(c)
        if c == 0:
            for cp in locals_[1:]:
                cp.wait()
        ring_copy(c, 3, 0).wait_recv()
        ring_copy(c, 3, 1).wait_recv()
        for e in range(2):
            grad = Pb[c, k, z, e].astype(F32) + Rr[c, 3, 0, e].astype(F32)
            grad = grad + Rr[c, 3, 1, e].astype(F32)
            w = wv[:, e, q]
            a = beta_one * m1v[:, e, q] + (1.0 - beta_one) * grad
            b = beta_two * m2v[:, e, q] + (1.0 - beta_two) * grad * grad
            update = a / bias_one / (jnp.sqrt(b / bias_two) + adam_epsilon) + decay_rate * w
            wv[:, e, q] = w - learn_rate * update
            m1v[:, e, q] = a
            m2v[:, e, q] = b
        nsx[c, 2 * zl + k] = wv[:, :, q].astype(BF16)
        for way in range(2):
            pl.when(z_sends(way, 0))(z_copy(c, way, 0).start)
        y_copy(c, zl).start()
        for cp in out_copies(c):
            cp.start()

    def z_forward(c, j):
        for way in range(2):
            shard = zl - j if way == 0 else zl + j

            @pl.when((shard >= 0) & (shard < 4))
            def _():
                z_copy(c, way, j - 1).wait_recv()
                if j < 3:
                    pl.when(z_sends(way, j))(z_copy(c, way, j).start)
                y_copy(c, shard).start()

    def z_end(c):
        for shard in range(4):
            y_copy(c, shard).wait_recv()
        ns_out(c).start()

    def send_back():
        at = lax.broadcasted_iota(jnp.int32, (2 * H, H), 0)
        column = lax.broadcasted_iota(jnp.int32, (2 * H, H), 1)
        for e in range(4):
            rows = slice(e % 2 * H, e % 2 * H + H)
            pick = jnp.where(at == 2 * column + e % 2, 1.0, 0.0).astype(BF16)
            G[e // 2, rows, 0:H] = jnp.dot(
                G[e // 2, rows, :].astype(BF16), pick, preferred_element_type=F32
            )

        def one(r, carry):
            s = lax.rem(own + r, 16)
            rows = [G[e // 2, pl.ds(e % 2 * H + s * CAP, CAP), 0:H] for e in range(4)]
            bs[s] = jnp.concatenate(rows, axis=0).astype(BF16)

            @pl.when(r < 16)
            def _():
                back_copy(r, s).start()

            return carry

        lax.fori_loop(1, 17, one, 0)
        pltpu.make_async_copy(bs.at[own], br.at[own], loc.at[7]).start()

    def finish():
        pltpu.make_async_copy(bs.at[own], br.at[own], loc.at[7]).wait()

        def arrive(r, carry):
            p = lax.rem(own + 16 - r, 16)
            remote(br.at[p], br.at[p], b_s.at[r], b_r.at[r], plane(p)).wait_recv()
            return carry

        lax.fori_loop(1, 16, arrive, 0)

        probs_out = []
        for n in range(8):
            g = jnp.dot(
                TT[n * 128 : (n + 1) * 128, :],
                br[...].reshape(EXPERTS * CAP, H),
                preferred_element_type=F32,
            )
            outf[:, n, :] = pc[:, n : n + 1] * g
            probs_out.append(jnp.sum(hid[:, n, :].astype(F32) * g, axis=1, keepdims=True))
        dpT[...] = jnp.transpose(jnp.concatenate(probs_out, axis=1))
        dh[...] = outf[...].astype(BF16)

    def pos_arrive(r, carry):
        p = lax.rem(own + 16 - r, 16)
        remote(posr.at[p], posr.at[p], pos_s.at[r], pos_r.at[r], plane(p)).wait_recv()
        return carry

    def w_arrive(r, carry):
        p = lax.rem(own + 16 - r, 16)
        remote(wr.at[p], wr.at[p], w_s.at[r], w_r.at[r], plane(p)).wait_recv()
        return carry

    g_start(0, 0)
    chain_begin(0)
    chain_begin(1)
    chain_begin(2)
    chain_begin(3)
    chain_begin(4)
    chain_begin(5)
    chain_begin(6)
    g_wait(0, 0)
    g_start(0, 1)
    chain_begin(7)
    choices()
    g_wait(0, 1)
    g_start(0, 2)
    build_rows()
    chain_step(0)
    send_rows(0)
    send_rows(1)
    send_rows(2)
    chain_step(1)
    send_rows(3)
    g_start(1, 0)
    g_start(2, 0)
    g_start(3, 0)
    g_start(4, 0)
    g_wait(0, 2)
    g_start(0, 3)
    build_M2()
    chain_step(2)
    build_TT()
    chain_step(3)
    chain_step(4)
    chain_step(5)
    g_wait(1, 0)
    g_start(1, 1)
    build_wT()
    g_wait(2, 0)
    g_start(2, 1)
    chain_step(6)
    g_wait(3, 0)
    g_start(3, 1)
    g_wait(4, 0)
    g_start(4, 1)
    g_wait(1, 1)
    g_start(1, 2)
    rows_of(0)
    g_wait(2, 1)
    g_start(2, 2)
    g_start(5, 0)
    partials(0)
    chain_step(7)
    hidden_grads(0)
    g_wait(1, 2)
    g_start(1, 3)
    g_wait(3, 1)
    g_start(3, 2)
    pair_sum(0)
    chain_step(8)
    g_wait(2, 2)
    g_start(2, 3)
    g_wait(4, 1)
    g_start(4, 2)
    ring_step(0, 1)
    g_wait(5, 0)
    g_start(5, 1)
    rows_of(1)
    chain_step(9)
    g_start(6, 0)
    partials(1)
    ring_step(0, 2)
    g_wait(3, 2)
    g_start(3, 3)
    hidden_grads(1)
    chain_step(10)
    rows_of(2)
    pair_sum(1)
    ring_step(0, 3)
    g_start(7, 0)
    g_wait(5, 1)
    g_start(5, 2)
    g_wait(4, 2)
    g_start(4, 3)
    g_wait(6, 0)
    g_start(6, 1)
    partials(2)
    ring_step(1, 1)
    hidden_grads(2)
    g_wait(7, 0)
    g_start(7, 1)
    adam(0)
    pair_sum(2)
    ring_step(1, 2)
    rows_of(3)
    g_wait(5, 2)
    g_start(5, 3)
    z_forward(0, 1)
    g_wait(6, 1)
    g_start(6, 2)
    g_wait(7, 1)
    g_start(7, 2)
    ring_step(2, 1)
    ring_step(1, 3)
    partials(3)
    z_forward(0, 2)
    hidden_grads(3)
    ring_step(2, 2)
    rows_of(4)
    pair_sum(3)
    g_wait(6, 2)
    g_start(6, 3)
    z_forward(0, 3)
    adam(1)
    ring_step(2, 3)
    ring_step(3, 1)
    g_wait(7, 2)
    g_start(7, 3)
    partials(4)
    z_forward(1, 1)
    hidden_grads(4)
    adam(2)
    pair_sum(4)
    ring_step(3, 2)
    rows_of(5)
    z_forward(1, 2)
    z_forward(2, 1)
    ring_step(4, 1)
    partials(5)
    ring_step(3, 3)
    hidden_grads(5)
    z_forward(1, 3)
    rows_of(6)
    pair_sum(5)
    ring_step(4, 2)
    z_forward(2, 2)
    adam(3)
    partials(6)
    ring_step(5, 1)
    ring_step(4, 3)
    hidden_grads(6)
    z_forward(2, 3)
    rows_of(7)
    pair_sum(6)
    ring_step(5, 2)
    z_forward(3, 1)
    partials(7)
    adam(4)
    ring_step(6, 1)
    ring_step(5, 3)
    hidden_grads(7)
    pair_sum(7)
    z_forward(3, 2)
    z_forward(4, 1)
    send_back()
    ring_step(6, 2)
    ring_step(7, 1)
    adam(5)
    z_forward(3, 3)
    z_end(0)
    z_forward(4, 2)
    z_end(1)
    z_end(2)
    ring_step(6, 3)
    z_end(3)
    ring_step(7, 2)
    z_forward(5, 1)
    z_forward(4, 3)
    adam(6)
    z_end(4)
    ring_step(7, 3)
    z_forward(5, 2)
    z_forward(6, 1)
    adam(7)
    z_forward(5, 3)
    z_forward(6, 2)
    z_end(5)
    z_forward(7, 1)
    z_forward(6, 3)
    z_forward(7, 2)
    z_end(6)
    finish()
    z_forward(7, 3)
    z_end(7)

    def sent(r, carry):
        p = lax.rem(own + r, 16)
        pos_copy(r, p).wait_send()
        w_copy(r, p).wait_send()
        back_copy(r, p).wait_send()
        return carry

    lax.fori_loop(1, 16, sent, 0)
    for c in range(NC):
        for n in range(16):
            gather_send(c, n).wait_send()
        for way in range(2):
            chain_sib(c, way).wait_send()
            for t in range(4):
                ring_copy(c, t, way).wait_send()
        chain(c, 0).wait_send()
        chain(c, 1).wait_send()
        pair_copy(c).wait_send()
        for way in range(2):
            for j in range(3):
                pl.when(z_sends(way, j))(z_copy(c, way, j).wait_send)
        for shard in range(4):
            y_copy(c, shard).wait_send()
        ns_out(c).wait()
        for cp in out_copies(c):
            cp.wait()


def local(cotangent, hidden, probs, expert_ids, secondary, weight, moment1, moment2):
    hbm = pl.BlockSpec(memory_space=pl.ANY)
    vmem = pl.BlockSpec(memory_space=pltpu.VMEM)
    dma = pltpu.SemaphoreType.DMA
    shape = jax.ShapeDtypeStruct
    dh, dpT, nw, nm1, nm2, ns = pl.pallas_call(
        body,
        out_shape=(
            shape((128, 8, H), BF16),
            shape((8, 128), F32),
            shape((48, 2, D), F32),
            shape((48, 2, D), F32),
            shape((48, 2, D), F32),
            shape((8, 48, 2, D), BF16),
        ),
        in_specs=[hbm, vmem, vmem] + [hbm] * 5,
        out_specs=(vmem, vmem, hbm, hbm, hbm, hbm),
        scratch_shapes=[
            pltpu.VMEM((4, 4, NC, 128, CW), BF16),
            pltpu.VMEM((2, NC, H, 2, CW), BF16),
            pltpu.VMEM((8, 8, 128), F32),
            pltpu.VMEM((16, 8, 128), F32),
            pltpu.VMEM((16, 4 * CAP, H), BF16),
            pltpu.VMEM((16, 4 * CAP, H), BF16),
            pltpu.VMEM((2, 2 * H, 2 * H), F32),
            pltpu.VMEM((4, H, H), BF16),
            pltpu.VMEM((8, 192, 256), BF16),
            pltpu.VMEM((2, 2 * H, CW), BF16),
            pltpu.VMEM((NC, 2, 8, 2, 48, CW), BF16),
            pltpu.VMEM((NC, 8, 2, 48, CW), BF16),
            pltpu.VMEM((NC, 4, 2, 2, 48, CW), BF16),
            pltpu.VMEM((16, 4 * CAP, H), BF16),
            pltpu.VMEM((16, 4 * CAP, H), BF16),
            pltpu.VMEM((1024, EXPERTS * CAP), BF16),
            pltpu.VMEM((EXPERTS * CAP, 1024), BF16),
            pltpu.VMEM((1024, H), BF16),
            pltpu.VMEM((128, 8, H), BF16),
            pltpu.VMEM((128, 8, H), F32),
            pltpu.VMEM((8, 128), F32),
            pltpu.VMEM((128, 8), F32),
            pltpu.VMEM((128, 8), F32),
            pltpu.VMEM((48, 2, D), F32),
            pltpu.VMEM((48, 2, D), F32),
            pltpu.VMEM((48, 2, D), F32),
            pltpu.VMEM((NC, 8, 48, 2, CW), BF16),
            dma((9 + 3 * NC,)), dma((2, NC)), dma((NC,)),
            dma((16,)), dma((16,)), dma((16,)), dma((16,)), dma((16,)), dma((16,)),
            dma((NC, 16)), dma((NC, 16)),
            dma((NC, 2)), dma((NC, 2)), dma((NC, 2)), dma((NC, 2)),
            dma((NC,)), dma((NC,)),
            dma((NC, 4, 2)), dma((NC, 4, 2)),
            dma((NC, 2, 3)), dma((NC, 2, 3)), dma((NC, 4)), dma((NC, 4)),
        ],
        compiler_params=pltpu.CompilerParams(
            collective_id=0, has_side_effects=True, vmem_limit_bytes=60 * 1024 * 1024
        ),
    )(cotangent, expert_ids.T, probs.T, hidden, secondary, weight, moment1, moment2)
    return dh, dpT.T, nw, nm1, nm2, ns.reshape(H, 2, D)


def solution(mesh):
    in_specs = (
        P(("outer", "inner"), None),
        P(("outer", "inner"), None, None),
        P(("outer", "inner"), None),
        P(("outer", "inner"), None),
        P(None, "inner", None),
        P("outer", "inner", None),
        P("outer", "inner", None),
        P("outer", "inner", None),
    )
    out_specs = (
        P(("outer", "inner"), None, None),
        P(("outer", "inner"), None),
        P("outer", "inner", None),
        P("outer", "inner", None),
        P("outer", "inner", None),
        P(None, "inner", None),
    )
    return jax.shard_map(local, mesh=mesh, in_specs=in_specs, out_specs=out_specs, check_vma=False)
```

```python
import functools

import jax
import jax.numpy as jnp
from jax import lax
from jax.experimental import pallas as pl
from jax.experimental.pallas import tpu as pltpu
from jax.sharding import PartitionSpec as P

EXPERTS = 64
CAP = 24
H = 384
D = 2048
NC = 4
CW = D // NC
MESH = pl.DeviceIdType.MESH
F32 = jnp.float32
BF16 = jnp.bfloat16

beta_one = 0.9
beta_two = 0.95
adam_epsilon = 1e-08
learn_rate = 0.003
decay_rate = 0.1
bias_one = 1.0 - 0.9**20
bias_two = 1.0 - 0.95**20


def body(
    cot_hbm, ids, prT, hid_hbm, sec_hbm, weight, moment1, moment2,
    dh, dpT, nw, nm1, nm2, ns,
    cot, sec, ps, posr, ws, wr, G, wT, M2, dsl, Pb, Ps, Rr, bs, br, TT, T, Wk, hid, outf,
    tgt, tgc, pc, wv, m1v, m2v, nsx,
    loc, in_s, out_s, pos_s, pos_r, w_s, w_r, b_s, b_r, ag_s, ag_r, sc_s, sc_r, sd_s, sd_r,
    pd_s, pd_r, rs_s, rs_r, z_s, z_r, y_s, y_r,
):
    o = lax.axis_index("outer")
    i = lax.axis_index("inner")
    k = lax.rem(o, 2)
    zl = lax.div(o, 2)
    zh = lax.rem(i, 2)
    own = lax.div(i, 2)
    x = lax.rem(own, 4)
    y = lax.div(own, 4)
    z = zh * 4 + zl

    def dev(px, py, pz, pk):
        return (lax.rem(pz, 4) * 2 + pk, (py * 4 + px) * 2 + lax.div(pz, 4))

    def plane(p):
        return (o, p * 2 + zh)

    xp, xm = lax.rem(x + 1, 4), lax.rem(x + 3, 4)
    yp, ym = lax.rem(y + 1, 4), lax.rem(y + 3, 4)
    zp, zm = lax.rem(z + 1, 8), lax.rem(z + 7, 8)
    dxp, dxm = dev(xp, y, z, k), dev(xm, y, z, k)
    dyp, dym = dev(x, yp, z, k), dev(x, ym, z, k)
    dzp, dzm = dev(x, y, zp, k), dev(x, y, zm, k)
    sib = (zl * 2 + 1 - k, i)

    def remote(src, dst, ss, rs, where):
        return pltpu.make_async_remote_copy(
            src_ref=src, dst_ref=dst, send_sem=ss, recv_sem=rs, device_id=where, device_id_type=MESH
        )

    barrier = pltpu.get_barrier_semaphore()

    def hello(r, c):
        pl.semaphore_signal(
            barrier, inc=1, device_id=plane(lax.rem(own + r, 16)), device_id_type=MESH
        )
        return c

    lax.fori_loop(1, 16, hello, 0)
    for where in (sib, dzp, dzm):
        pl.semaphore_signal(barrier, inc=1, device_id=where, device_id_type=MESH)

    locals_ = [
        pltpu.make_async_copy(hid_hbm, hid, loc.at[2]),
        pltpu.make_async_copy(weight, wv, loc.at[4]),
        pltpu.make_async_copy(moment1, m1v, loc.at[5]),
        pltpu.make_async_copy(moment2, m2v, loc.at[6]),
    ]
    def cols(c):
        return pl.ds(c * CW if isinstance(c, int) else pl.multiple_of(c * CW, CW), CW)

    def cot_in(c):
        return pltpu.make_async_copy(cot_hbm.at[:, cols(c)], cot.at[y, x, c], in_s.at[0, c])

    def sec_in(c):
        return pltpu.make_async_copy(sec_hbm.at[:, :, cols(c)], sec.at[zh, c], in_s.at[1, c])

    for c in range(NC):
        cot_in(c).start()
        sec_in(c).start()
    for cp in locals_:
        cp.start()

    def rank_choices():
        named = ids[...]
        experts = lax.broadcasted_iota(jnp.int32, (EXPERTS, 128), 0)
        hits = [named[n : n + 1, :] == experts for n in range(8)]
        chosen = functools.reduce(jnp.logical_or, hits)
        first = lax.broadcasted_iota(jnp.int32, (128, 128), 0)
        second = lax.broadcasted_iota(jnp.int32, (128, 128), 1)
        before = jnp.where(first < second, 1.0, 0.0).astype(BF16)
        rank = jnp.dot(
            jnp.where(chosen, 1.0, 0.0).astype(BF16), before, preferred_element_type=F32
        )
        ps[...] = jnp.where(chosen, rank, -1.0).reshape(8, 8, 128)
        place = rank + (experts * CAP).astype(F32)
        rows = [jnp.sum(jnp.where(hit, place, 0.0), axis=0, keepdims=True) for hit in hits]
        target = jnp.concatenate(rows, axis=0)
        tgt[...] = target
        tgc[...] = jnp.transpose(target)
        pc[...] = jnp.transpose(prT[...])

    rank_choices()
    pl.semaphore_wait(barrier, 18)

    def pos_copy(r, p):
        return remote(ps.at[lax.div(p, 2)], posr.at[own], pos_s.at[r], pos_r.at[r], plane(p))

    def w_copy(r, p):
        return remote(ws.at[p], wr.at[own], w_s.at[r], w_r.at[r], plane(p))

    def back_copy(r, p):
        return remote(bs.at[p], br.at[own], b_s.at[r], b_r.at[r], plane(p))

    A, B = pl.ds(0, 64), pl.ds(64, 64)
    A0, A1, B0, B1 = pl.ds(0, 32), pl.ds(32, 32), pl.ds(64, 32), pl.ds(96, 32)

    def gather_send(c, n):
        q = cols(c)
        spec = (
            (cot_hbm.at[A, q], cot.at[y, x, c, A], dxp),
            (cot_hbm.at[A, q], cot.at[y, x, c, A], dxm),
            (cot_hbm.at[B, q], cot.at[y, x, c, B], dyp),
            (cot_hbm.at[B, q], cot.at[y, x, c, B], dym),
            (cot.at[y, xm, c, A0],) * 2 + (dxp,),
            (cot.at[y, xp, c, A1],) * 2 + (dxm,),
            (cot.at[ym, x, c, B0],) * 2 + (dyp,),
            (cot.at[yp, x, c, B1],) * 2 + (dym,),
            (cot.at[y, :, c, A],) * 2 + (dyp,),
            (cot.at[y, :, c, A],) * 2 + (dym,),
            (cot.at[:, x, c, B],) * 2 + (dxp,),
            (cot.at[:, x, c, B],) * 2 + (dxm,),
            (cot.at[ym, :, c, A0],) * 2 + (dyp,),
            (cot.at[yp, :, c, A1],) * 2 + (dym,),
            (cot.at[:, xm, c, B0],) * 2 + (dxp,),
            (cot.at[:, xp, c, B1],) * 2 + (dxm,),
        )[n]
        return remote(spec[0], spec[1], ag_s.at[c, n], ag_r.at[c, n], spec[2])

    def g_start(c, stage):
        if stage == 2:
            cot_in(c).wait()
        for n in range(4 * stage, 4 * stage + 4):
            gather_send(c, n).start()

    def g_wait(c, stage):
        for n in range(4 * stage, 4 * stage + 4):
            gather_send(c, n).wait_recv()

    q_up = 1 - lax.div(zp, 4)
    q_dn = 1 - lax.div(zm, 4)
    other = 1 - zh
    quarter = [pl.ds(pl.multiple_of((k * 2 + way) * 96, 96), 96) for way in range(2)]

    def chain(c, way):
        ref = sec.at[(q_up, q_dn)[way], c, quarter[way]]
        return remote(ref, ref, sc_s.at[c, way], sc_r.at[c, way], (dzp, dzm)[way])

    def chain_sib(c, way):
        ref = sec.at[other, c, quarter[way]]
        return remote(ref, ref, sd_s.at[c, way], sd_r.at[c, way], sib)

    def chain_begin(c):
        sec_in(c).wait()

        @pl.when(zl == 3)
        def _():
            chain(c, 0).start()

        @pl.when(zl == 0)
        def _():
            chain(c, 1).start()

    def chain_step(slot):
        up, dn = slot - zl, slot - 3 + zl

        @pl.when((up >= 0) & (up < NC))
        def _():
            chain(up, 0).wait_recv()

            @pl.when(zl < 3)
            def _():
                chain(up, 0).start()

            chain_sib(up, 0).start()

        @pl.when((dn >= 0) & (dn < NC))
        def _():
            chain(dn, 1).wait_recv()

            @pl.when(zl > 0)
            def _():
                chain(dn, 1).start()

            chain_sib(dn, 1).start()

    def chain_end(c):
        chain_sib(c, 0).wait_recv()
        chain_sib(c, 1).wait_recv()

    def choices():
        pltpu.make_async_copy(ps.at[lax.div(own, 2)], posr.at[own], loc.at[3]).start()

        def one(r, carry):
            pos_copy(r, lax.rem(own + r, 16)).start()
            return carry

        lax.fori_loop(1, 16, one, 0)

    def build_rows():
        def one(b, carry):
            rows = pl.ds(b * 128, 128)
            slot = (lax.broadcasted_iota(jnp.int32, (128, 128), 0) + b * 128).astype(F32)
            for n in range(8):
                hit = slot == tgt[n : n + 1, :]
                T[rows, n * 128 : (n + 1) * 128] = jnp.where(hit, 1.0, 0.0).astype(BF16)
            return carry

        lax.fori_loop(0, 12, one, 0)
        locals_[0].wait()
        for n in range(8):
            rows = pc[:, n : n + 1] * hid[:, n, :].astype(F32)
            Wk[n * 128 : (n + 1) * 128, :] = rows.astype(BF16)

    def send_rows(n):
        ry = lax.rem(y + n + 1, 4)
        rows = pl.ds(pl.multiple_of(ry * 384, 384), 384)
        block = jnp.dot(T[rows, :], Wk[...], preferred_element_type=F32)
        ws[pl.ds(ry * 4, 4)] = block.astype(BF16).reshape(4, 4 * CAP, H)
        for m in range(4):
            p = ry * 4 + lax.rem(x + m, 4)
            if n == 3 and m == 0:
                pltpu.make_async_copy(ws.at[own], wr.at[own], loc.at[8]).start()
            else:
                w_copy(lax.rem(p - own + 16, 16), p).start()

    def build_TT():
        slot = lax.broadcasted_iota(jnp.int32, (128, EXPERTS * CAP), 1).astype(F32)
        for n in range(8):
            hit = slot == tgc[:, n : n + 1]
            TT[n * 128 : (n + 1) * 128, :] = jnp.where(hit, 1.0, 0.0).astype(BF16)

    def build_M2():
        lax.fori_loop(1, 16, pos_arrive, 0)
        pltpu.make_async_copy(ps.at[lax.div(own, 2)], posr.at[own], loc.at[3]).wait()
        odd = lax.rem(own, 2) == 1

        def one(b, carry):
            j = lax.broadcasted_iota(jnp.int32, (CAP, 128), 0).astype(F32)
            zero = jnp.zeros((CAP, 128), F32)
            first, second = (
                jnp.where(odd, part[4:8, :], part[0:4, :])
                for part in (posr[2 * b], posr[2 * b + 1])
            )
            rows = []
            for q in range(4):
                one_a = jnp.where(first[q : q + 1, :] == j, 1.0, 0.0)
                one_b = jnp.where(second[q : q + 1, :] == j, 1.0, 0.0)
                rows.append(jnp.concatenate([one_a, zero], axis=1))
                rows.append(jnp.concatenate([zero, one_b], axis=1))
            M2[b] = jnp.concatenate(rows, axis=0).astype(BF16)
            return carry

        lax.fori_loop(0, 8, one, 0)

    def build_wT():
        lax.fori_loop(1, 16, w_arrive, 0)
        pltpu.make_async_copy(ws.at[own], wr.at[own], loc.at[8]).wait()

        def one(s, carry):
            block = wr[s].astype(F32)
            for q in range(4):
                G[q // 2, pl.ds(q % 2 * H + s * CAP, CAP), 0:H] = block[q * CAP : (q + 1) * CAP, :]
            return carry

        lax.fori_loop(0, 16, one, 0)
        for q in range(4):
            wT[q] = jnp.transpose(G[q // 2, q % 2 * H : q % 2 * H + H, 0:H]).astype(BF16)

    def rows_of(c):
        g_wait(c, 3)

        def one(b, carry):
            block = cot[lax.div(b, 2), pl.ds(lax.rem(b, 2) * 2, 2), c].reshape(256, CW)
            got = jnp.dot(M2[b], block, preferred_element_type=F32).astype(BF16)
            for e in range(4):
                dsl[e // 2, pl.ds(e % 2 * H + b * 48, 48), :] = got[e * 48 : (e + 1) * 48, :]
            return carry

        lax.fori_loop(0, 8, one, 0)

    def partials(c):
        for e in range(4):
            got = jnp.dot(
                wT[e], dsl[e // 2, e % 2 * H : e % 2 * H + H, :], preferred_element_type=F32).astype(BF16)
            for s in range(8):
                Pb[c, s % 2, (e // 2) * 4 + s // 2, e % 2] = got[s * 48 : (s + 1) * 48, :]
        pair_copy(c).start()

    def hidden_grads(c):
        chain_end(c)
        for e in range(4):
            rows = slice(e % 2 * H, e % 2 * H + H)
            got = lax.dot_general(
                dsl[e // 2, rows, :],
                sec[e // 2, c].reshape(2 * H, CW),
                (((1,), (1,)), ((), ())),
                preferred_element_type=F32,
            )
            G[e // 2, rows, :] = got if c == 0 else G[e // 2, rows, :] + got

    def pair_copy(c):
        return remote(Pb.at[c, 1 - k], Ps.at[c], pd_s.at[c], pd_r.at[c], sib)

    def ring_copy(c, t, way):
        far = 4 - t
        d = lax.rem(z + far, 8) if way == 0 else lax.rem(z + 8 - far, 8)
        where = dzp if way == 0 else dzm
        if t == 0:
            src, dst = Pb.at[c, k, d, way], Rr.at[c, t, way, way]
        else:
            src, dst = Pb.at[c, k, d], Rr.at[c, t, way]
        return remote(src, dst, rs_s.at[c, t, way], rs_r.at[c, t, way], where)

    def pair_sum(c):
        pair_copy(c).wait_recv()
        Pb[c, k] = (Pb[c, k].astype(F32) + Ps[c].astype(F32)).astype(BF16)
        ring_copy(c, 0, 0).start()
        ring_copy(c, 0, 1).start()

    def ring_step(c, t):
        for way in range(2):
            far = 4 - t
            d = lax.rem(z + far, 8) if way == 0 else lax.rem(z + 8 - far, 8)
            ring_copy(c, t - 1, way).wait_recv()
            if t == 1:
                Pb[c, k, d, way] = (
                    Pb[c, k, d, way].astype(F32) + Rr[c, 0, way, way].astype(F32)
                ).astype(BF16)
            else:
                Pb[c, k, d] = (Pb[c, k, d].astype(F32) + Rr[c, t - 1, way].astype(F32)).astype(BF16)
            ring_copy(c, t, way).start()

    def z_copy(c, way, j):
        shard = jnp.maximum(zl - j, 0) if way == 0 else jnp.minimum(zl + j, 3)
        ref = nsx.at[c, 2 * shard + k]
        return remote(ref, ref, z_s.at[c, way, j], z_r.at[c, way, j], (dzp, dzm)[way])

    def z_sends(way, j):
        return ((zl >= j) & (zl < 3)) if way == 0 else ((zl + j <= 3) & (zl > 0))

    def y_copy(c, shard):
        ref = nsx.at[c, 2 * shard + k]
        return remote(ref, ref, y_s.at[c, shard], y_r.at[c, shard], sib)

    def ns_out(c):
        return pltpu.make_async_copy(nsx.at[c], ns.at[:, :, :, cols(c)], out_s.at[c])

    def out_copies(c):
        q = cols(c)
        return [
            pltpu.make_async_copy(v.at[:, :, q], dst.at[:, :, q], loc.at[9 + 3 * c + n])
            for n, (v, dst) in enumerate(((wv, nw), (m1v, nm1), (m2v, nm2)))
        ]

    def adam(c):
        q = cols(c)
        if c == 0:
            for cp in locals_[1:]:
                cp.wait()
        ring_copy(c, 3, 0).wait_recv()
        ring_copy(c, 3, 1).wait_recv()
        for e in range(2):
            grad = Pb[c, k, z, e].astype(F32) + Rr[c, 3, 0, e].astype(F32)
            grad = grad + Rr[c, 3, 1, e].astype(F32)
            w = wv[:, e, q]
            a = beta_one * m1v[:, e, q] + (1.0 - beta_one) * grad
            b = beta_two * m2v[:, e, q] + (1.0 - beta_two) * grad * grad
            update = a / bias_one / (jnp.sqrt(b / bias_two) + adam_epsilon) + decay_rate * w
            wv[:, e, q] = w - learn_rate * update
            m1v[:, e, q] = a
            m2v[:, e, q] = b
        nsx[c, 2 * zl + k] = wv[:, :, q].astype(BF16)
        for way in range(2):
            pl.when(z_sends(way, 0))(z_copy(c, way, 0).start)
        y_copy(c, zl).start()
        for cp in out_copies(c):
            cp.start()

    def z_forward(c, j):
        for way in range(2):
            shard = zl - j if way == 0 else zl + j

            @pl.when((shard >= 0) & (shard < 4))
            def _():
                z_copy(c, way, j - 1).wait_recv()
                if j < 3:
                    pl.when(z_sends(way, j))(z_copy(c, way, j).start)
                y_copy(c, shard).start()

    def z_end(c):
        for shard in range(4):
            y_copy(c, shard).wait_recv()
        ns_out(c).start()
        for way in range(2):
            for t in range(4):
                ring_copy(c, t, way).wait_send()
            for j in range(3):
                pl.when(z_sends(way, j))(z_copy(c, way, j).wait_send)
        pair_copy(c).wait_send()
        for shard in range(4):
            y_copy(c, shard).wait_send()
        for cp in out_copies(c):
            cp.wait()

    def back_sent(r, carry):
        back_copy(r, lax.rem(own + r, 16)).wait_send()
        return carry

    def early_sent():
        def one(r, carry):
            p = lax.rem(own + r, 16)
            pos_copy(r, p).wait_send()
            w_copy(r, p).wait_send()
            return carry

        lax.fori_loop(1, 16, one, 0)
        for c in range(NC):
            for n in range(16):
                gather_send(c, n).wait_send()
            for way in range(2):
                chain_sib(c, way).wait_send()
                chain(c, way).wait_send()

    def send_back():
        at = lax.broadcasted_iota(jnp.int32, (2 * H, H), 0)
        column = lax.broadcasted_iota(jnp.int32, (2 * H, H), 1)
        for e in range(4):
            rows = slice(e % 2 * H, e % 2 * H + H)
            pick = jnp.where(at == 2 * column + e % 2, 1.0, 0.0).astype(BF16)
            G[e // 2, rows, 0:H] = jnp.dot(
                G[e // 2, rows, :].astype(BF16), pick, preferred_element_type=F32
            )

        def one(r, carry):
            s = lax.rem(own + r, 16)
            rows = [G[e // 2, pl.ds(e % 2 * H + s * CAP, CAP), 0:H] for e in range(4)]
            bs[s] = jnp.concatenate(rows, axis=0).astype(BF16)

            @pl.when(r < 16)
            def _():
                back_copy(r, s).start()

            return carry

        lax.fori_loop(1, 17, one, 0)
        pltpu.make_async_copy(bs.at[own], br.at[own], loc.at[7]).start()

    def finish():
        pltpu.make_async_copy(bs.at[own], br.at[own], loc.at[7]).wait()

        def arrive(r, carry):
            p = lax.rem(own + 16 - r, 16)
            remote(br.at[p], br.at[p], b_s.at[r], b_r.at[r], plane(p)).wait_recv()
            return carry

        lax.fori_loop(1, 16, arrive, 0)

        probs_out = []
        for n in range(8):
            g = jnp.dot(
                TT[n * 128 : (n + 1) * 128, :],
                br[...].reshape(EXPERTS * CAP, H),
                preferred_element_type=F32,
            )
            outf[:, n, :] = pc[:, n : n + 1] * g
            probs_out.append(jnp.sum(hid[:, n, :].astype(F32) * g, axis=1, keepdims=True))
        dpT[...] = jnp.transpose(jnp.concatenate(probs_out, axis=1))
        dh[...] = outf[...].astype(BF16)

    def pos_arrive(r, carry):
        p = lax.rem(own + 16 - r, 16)
        remote(posr.at[p], posr.at[p], pos_s.at[r], pos_r.at[r], plane(p)).wait_recv()
        return carry

    def w_arrive(r, carry):
        p = lax.rem(own + 16 - r, 16)
        remote(wr.at[p], wr.at[p], w_s.at[r], w_r.at[r], plane(p)).wait_recv()
        return carry

    chain_begin(0)
    chain_begin(1)
    chain_begin(2)
    chain_begin(3)
    g_start(0, 0)
    choices()
    g_wait(0, 0)
    g_start(0, 1)
    build_TT()
    chain_step(0)
    g_wait(0, 1)
    g_start(0, 2)
    build_rows()
    send_rows(0)
    send_rows(1)
    send_rows(2)
    chain_step(1)
    send_rows(3)
    g_start(1, 0)
    g_wait(0, 2)
    g_start(0, 3)
    g_start(2, 0)
    build_M2()
    chain_step(2)
    chain_step(3)
    build_wT()
    g_wait(1, 0)
    g_start(1, 1)
    chain_step(4)
    rows_of(0)
    g_wait(1, 1)
    g_start(1, 2)
    partials(0)
    g_wait(2, 0)
    g_start(2, 1)
    chain_step(5)
    g_start(3, 0)
    hidden_grads(0)
    pair_sum(0)
    g_wait(1, 2)
    g_start(1, 3)
    g_wait(2, 1)
    g_start(2, 2)
    chain_step(6)
    g_wait(3, 0)
    g_start(3, 1)
    ring_step(0, 1)
    rows_of(1)
    partials(1)
    hidden_grads(1)
    g_wait(3, 1)
    g_start(3, 2)
    ring_step(0, 2)
    g_wait(2, 2)
    g_start(2, 3)
    pair_sum(1)
    ring_step(0, 3)
    ring_step(1, 1)
    g_wait(3, 2)
    g_start(3, 3)
    adam(0)
    rows_of(2)
    ring_step(1, 2)
    partials(2)
    z_forward(0, 1)
    hidden_grads(2)
    ring_step(1, 3)
    rows_of(3)
    partials(3)
    z_forward(0, 2)
    pair_sum(2)
    adam(1)
    hidden_grads(3)
    ring_step(2, 1)
    z_forward(0, 3)
    pair_sum(3)
    z_forward(1, 1)
    send_back()
    ring_step(2, 2)
    ring_step(3, 1)
    z_end(0)
    z_forward(1, 2)
    ring_step(2, 3)
    ring_step(3, 2)
    z_forward(1, 3)
    z_end(1)
    adam(2)
    ring_step(3, 3)
    z_forward(2, 1)
    adam(3)
    early_sent()
    finish()
    z_forward(2, 2)
    z_forward(3, 1)
    z_forward(2, 3)
    z_end(2)
    z_forward(3, 2)
    z_forward(3, 3)
    z_end(3)

    lax.fori_loop(1, 16, back_sent, 0)
    for c in range(NC):
        ns_out(c).wait()


def local(cotangent, hidden, probs, expert_ids, secondary, weight, moment1, moment2):
    hbm = pl.BlockSpec(memory_space=pl.ANY)
    vmem = pl.BlockSpec(memory_space=pltpu.VMEM)
    dma = pltpu.SemaphoreType.DMA
    shape = jax.ShapeDtypeStruct
    dh, dpT, nw, nm1, nm2, ns = pl.pallas_call(
        body,
        out_shape=(
            shape((128, 8, H), BF16),
            shape((8, 128), F32),
            shape((48, 2, D), F32),
            shape((48, 2, D), F32),
            shape((48, 2, D), F32),
            shape((8, 48, 2, D), BF16),
        ),
        in_specs=[hbm, vmem, vmem] + [hbm] * 5,
        out_specs=(vmem, vmem, hbm, hbm, hbm, hbm),
        scratch_shapes=[
            pltpu.VMEM((4, 4, NC, 128, CW), BF16),
            pltpu.VMEM((2, NC, H, 2, CW), BF16),
            pltpu.VMEM((8, 8, 128), F32),
            pltpu.VMEM((16, 8, 128), F32),
            pltpu.VMEM((16, 4 * CAP, H), BF16),
            pltpu.VMEM((16, 4 * CAP, H), BF16),
            pltpu.VMEM((2, 2 * H, 2 * H), F32),
            pltpu.VMEM((4, H, H), BF16),
            pltpu.VMEM((8, 192, 256), BF16),
            pltpu.VMEM((2, 2 * H, CW), BF16),
            pltpu.VMEM((NC, 2, 8, 2, 48, CW), BF16),
            pltpu.VMEM((NC, 8, 2, 48, CW), BF16),
            pltpu.VMEM((NC, 4, 2, 2, 48, CW), BF16),
            pltpu.VMEM((16, 4 * CAP, H), BF16),
            pltpu.VMEM((16, 4 * CAP, H), BF16),
            pltpu.VMEM((1024, EXPERTS * CAP), BF16),
            pltpu.VMEM((EXPERTS * CAP, 1024), BF16),
            pltpu.VMEM((1024, H), BF16),
            pltpu.VMEM((128, 8, H), BF16),
            pltpu.VMEM((128, 8, H), F32),
            pltpu.VMEM((8, 128), F32),
            pltpu.VMEM((128, 8), F32),
            pltpu.VMEM((128, 8), F32),
            pltpu.VMEM((48, 2, D), F32),
            pltpu.VMEM((48, 2, D), F32),
            pltpu.VMEM((48, 2, D), F32),
            pltpu.VMEM((NC, 8, 48, 2, CW), BF16),
            dma((9 + 3 * NC,)), dma((2, NC)), dma((NC,)),
            dma((16,)), dma((16,)), dma((16,)), dma((16,)), dma((16,)), dma((16,)),
            dma((NC, 16)), dma((NC, 16)),
            dma((NC, 2)), dma((NC, 2)), dma((NC, 2)), dma((NC, 2)),
            dma((NC,)), dma((NC,)),
            dma((NC, 4, 2)), dma((NC, 4, 2)),
            dma((NC, 2, 3)), dma((NC, 2, 3)), dma((NC, 4)), dma((NC, 4)),
        ],
        compiler_params=pltpu.CompilerParams(
            collective_id=0, has_side_effects=True, vmem_limit_bytes=60 * 1024 * 1024
        ),
    )(cotangent, expert_ids.T, probs.T, hidden, secondary, weight, moment1, moment2)
    return dh, dpT.T, nw, nm1, nm2, ns.reshape(H, 2, D)


def solution(mesh):
    in_specs = (
        P(("outer", "inner"), None),
        P(("outer", "inner"), None, None),
        P(("outer", "inner"), None),
        P(("outer", "inner"), None),
        P(None, "inner", None),
        P("outer", "inner", None),
        P("outer", "inner", None),
        P("outer", "inner", None),
    )
    out_specs = (
        P(("outer", "inner"), None, None),
        P(("outer", "inner"), None),
        P("outer", "inner", None),
        P("outer", "inner", None),
        P("outer", "inner", None),
        P(None, "inner", None),
    )
    return jax.shard_map(local, mesh=mesh, in_specs=in_specs, out_specs=out_specs, check_vma=False)
```
